512 devices in a mesh: blk: 64 (over x, z_lo, y), uly: 8 (over z_hi, core).
Axes of the slice: x: 4, y: 8, z: 8 (z_hi: 4, z_lo: 2; z = z_hi * 2 + z_lo), core: 2. Of those that a mesh axis runs over, the one named last changes fastest.
Arguments:
- query_rows: bfloat16 [32768, 5120], P(('blk', 'uly')), may hold values from -6 to 6
- key_rows: bfloat16 [32768, 5120], P(('blk', 'uly')), may hold values from -6 to 6
- value_rows: bfloat16 [32768, 5120], P(('blk', 'uly')), may hold values from -6 to 6
- out_grad: bfloat16 [32768, 5120], P(('blk', 'uly')), may hold values from -96 to 96
- log_sums: bfloat16 [32768, 40], P(('blk', 'uly')), as said below
- deltas: bfloat16 [32768, 40], P(('blk', 'uly')), may hold values from -900 to 900
Outputs:
- grad_query: bfloat16 [32768, 5120], P(('blk', 'uly'))
- grad_key: bfloat16 [32768, 5120], P(('blk', 'uly'))
- grad_value: bfloat16 [32768, 5120], P(('blk', 'uly'))
The draws below stay inside these ranges and needn't reach their ends.
Inputs may be any that keep to these rules, and one draw needn't show every extreme that they name: `log_sums`: each value lies within 1 of log(1024) + 0.5.
All inputs are finite; a program needn't handle non-finite values.
Results may differ from the reference program's by a relative error of at most 0.0058.
Values may be sent and summed in bfloat16 or wider, within the bound.
No kernel may reach another device: no remote copies, remote signals or barrier semaphores. Data moves between devices by JAX's collectives and lax.ppermute only.
A program may use at most 64 MiB of HBM per device.

```python
import math
import jax
import jax.numpy as jnp
from jax import lax

HD = 128
SEQ_BLK = 512
HEADS = 40
SEQ = 32768
N_BLK = 64


def draw_log_sums(key, part):
    key = jax.random.fold_in(key, 11)
    center = math.log(2.0 * SEQ_BLK) + 0.5
    values = center + jax.random.uniform(key, (SEQ, HEADS), jnp.float32, -1.0, 1.0)
    return values.astype(jnp.bfloat16)


def levels(key, dims, split, smallest, largest):
    level = 1.0
    for position, blocks in split:
        heights = jax.random.uniform(jax.random.fold_in(jax.random.fold_in(key, 6), position), (blocks,), jnp.float32, smallest / len(split), largest / len(split))
        level = level * jnp.repeat(jnp.exp(heights), dims[position] // blocks).reshape((-1,) + (1,) * (len(dims) - 1 - position))
    return level


def bell_draw(own_key, extent, scale, bound, shards=(), held_as=jnp.bfloat16):
    factor_of = levels(own_key, extent, shards, -0.22, 0.18) if shards else 1.0
    entries = jax.random.normal(own_key, extent, jnp.float32) * scale * factor_of
    return jnp.minimum(jnp.maximum(entries, -bound), bound).astype(held_as)


def setup_inputs(seed: int = 0) -> dict:
    seeds = jax.random.split(jax.random.key(seed), 7)
    query_rows = bell_draw(seeds[0], (SEQ, HEADS * HD), 1.0, 6.0, ((0, 512),))
    key_rows = bell_draw(seeds[1], (SEQ, HEADS * HD), 1.0, 6.0, ((0, 512),))
    value_rows = bell_draw(seeds[2], (SEQ, HEADS * HD), 1.0, 6.0, ((0, 512),))
    out_grad = bell_draw(seeds[3], (SEQ, HEADS * HD), 16.0, 96.0, ((0, 512),))
    log_sums = draw_log_sums(jax.random.fold_in(seeds[6], 71), 0)
    deltas = bell_draw(seeds[5], (SEQ, HEADS), 150.0, 900.0, ((0, 512),))
    return dict(query_rows=query_rows, key_rows=key_rows, value_rows=value_rows, out_grad=out_grad, log_sums=log_sums, deltas=deltas)


def block_grads(qb, gb, lb, db, kb, vb, scale):
    f32 = jnp.float32
    score = jnp.einsum("qhd,khd->hqk", qb.astype(f32), kb.astype(f32)) * scale
    prob = jnp.exp(score - jnp.transpose(lb.astype(f32))[:, :, None])
    prob_low = prob.astype(jnp.bfloat16)
    grad_value = jnp.einsum("hqk,qhd->khd", prob_low.astype(f32), gb.astype(f32))
    grad_prob = jnp.einsum("qhd,khd->hqk", gb.astype(f32), vb.astype(f32))
    grad_score = (prob * (grad_prob - jnp.transpose(db.astype(f32))[:, :, None])).astype(jnp.bfloat16)
    grad_query = jnp.einsum("hqk,khd->qhd", grad_score.astype(f32), kb.astype(f32)) * scale
    grad_key = jnp.einsum("hqk,qhd->khd", grad_score.astype(f32), qb.astype(f32)) * scale
    return grad_query, grad_key, grad_value


def reference(query_rows, key_rows, value_rows, out_grad, log_sums, deltas):
    scale = HD ** -0.5
    blocks = (N_BLK, SEQ_BLK, HEADS, HD)
    queries = query_rows.reshape(blocks)
    keys_all = key_rows.reshape(blocks)
    values_all = value_rows.reshape(blocks)
    grads_out = out_grad.reshape(blocks)
    sums_all = log_sums.reshape(N_BLK, SEQ_BLK, HEADS)
    delta_all = deltas.reshape(N_BLK, SEQ_BLK, HEADS)
    keys_next = jnp.roll(keys_all, -1, axis=0)
    values_next = jnp.roll(values_all, -1, axis=0)

    def one_block(items):
        qb, gb, lb, db, kb, vb, kc, vc = items
        own = block_grads(qb, gb, lb, db, kb, vb, scale)
        cross = block_grads(qb, gb, lb, db, kc, vc, scale)
        return own[0] + cross[0], own[1], own[2], cross[1], cross[2]

    grad_q, key_own, value_own, key_cross, value_cross = lax.map(
        one_block, (queries, grads_out, sums_all, delta_all, keys_all, values_all, keys_next, values_next))
    grad_k = key_own + jnp.roll(key_cross, 1, axis=0)
    grad_v = value_own + jnp.roll(value_cross, 1, axis=0)
    shape2 = (SEQ, HEADS * HD)
    return (grad_q.astype(jnp.bfloat16).reshape(shape2),
            grad_k.astype(jnp.bfloat16).reshape(shape2),
            grad_v.astype(jnp.bfloat16).reshape(shape2))
```

```python
import functools

import jax
import jax.numpy as jnp
from jax import lax
from jax.experimental import pallas as pl
from jax.experimental.pallas import tpu as pltpu
from jax.sharding import PartitionSpec as P

F32 = jnp.float32
LOW = jnp.bfloat16
AXES = ("blk", "uly")
CHIPS = 4
RING = 8
NEVER = (RING,) * 8
SWAP_FROM = (2, 6, 2, 6, 2, 6, 2, 6)
PAD = 16


def holder(b, u):
    return b ^ RING if b % RING >= SWAP_FROM[u] else b


def gather_pairs(blocks, d):
    pairs = []
    for b in range(blocks):
        for u in range(2 * CHIPS):
            v = (u + 2 * d) % (2 * CHIPS)
            pairs.append((b * 8 + u, holder(b, v) * 8 + v))
    return pairs


def next_pairs(blocks):
    return [
        (holder(b, u) * 8 + u, holder((b + 1) % blocks, u) * 8 + u)
        for b in range(blocks)
        for u in range(8)
    ]


def back(pairs):
    return [(t, s) for s, t in pairs]


def core_pairs(blocks):
    return [(i, i ^ 1) for i in range(blocks * 8)]


def moved(value, pairs):
    if all(s == t for s, t in pairs):
        return value
    return lax.ppermute(value, AXES, pairs)


def whole(n):
    return [pl.BlockSpec(memory_space=pltpu.VMEM)] * n


def columns(group, width):
    return pl.ds(pl.multiple_of(group * width, 128), width)


def call(kernel, out_shape, place, *arrays, flops=0):
    moved_bytes = sum(a.size * a.dtype.itemsize for a in arrays)
    outs = out_shape if isinstance(out_shape, (list, tuple)) else [out_shape]
    moved_bytes += sum(o.size * o.dtype.itemsize for o in outs)
    return pl.pallas_call(
        kernel,
        out_shape=out_shape,
        in_specs=[pl.BlockSpec(memory_space=pltpu.SMEM)] + whole(len(arrays)),
        out_specs=jax.tree.map(lambda _: pl.BlockSpec(memory_space=pltpu.VMEM), out_shape),
        compiler_params=pltpu.CompilerParams(vmem_limit_bytes=32 << 20),
        cost_estimate=pl.CostEstimate(flops=flops, bytes_accessed=moved_bytes, transcendentals=0),
    )(place, *arrays)


def other_core_parts(first, second, stats, place):
    rows, width = first.shape[0], first.shape[1] // 8
    extra = PAD if stats is not None else 0

    def kernel(place_ref, a_ref, b_ref, *refs):
        out_ref = refs[-1]
        for d in range(CHIPS):
            group = 2 * lax.rem(place_ref[0] + d, CHIPS) + 1 - place_ref[1]
            out_ref[d, :rows] = a_ref[:, columns(group, width)]
            out_ref[d, rows : 2 * rows] = b_ref[:, columns(group, width)]
            if extra:
                out_ref[d, 2 * rows :] = refs[0][group]

    arrays = (first, second) + ((stats,) if extra else ())
    shape = jax.ShapeDtypeStruct((CHIPS, 2 * rows + extra, width), LOW)
    return call(kernel, shape, place, *arrays)


def messages(first, second, stats, other, place):
    rows, width = first.shape[0], first.shape[1] // 8
    extra = PAD if stats is not None else 0

    def kernel(place_ref, a_ref, b_ref, *refs):
        other_ref, outs = refs[-CHIPS - 1], refs[-CHIPS:]
        for d in range(CHIPS):
            group = 2 * lax.rem(place_ref[0] + d, CHIPS) + place_ref[1]
            outs[d][:rows] = a_ref[:, columns(group, width)]
            outs[d][rows : 2 * rows] = b_ref[:, columns(group, width)]
            outs[d][2 * rows : 4 * rows] = other_ref[d, : 2 * rows]
            if extra:
                outs[d][4 * rows :] = jnp.concatenate(
                    [refs[0][group, : PAD // 2], other_ref[d, 2 * rows : 2 * rows + PAD // 2]], axis=0
                )

    arrays = (first, second) + ((stats,) if extra else ()) + (other,)
    shape = [jax.ShapeDtypeStruct((4 * rows + extra, width), LOW)] * CHIPS
    return call(kernel, shape, place, *arrays)


def held(value, *first):
    return pl.pallas_call(
        lambda *refs: None,
        out_shape=jax.ShapeDtypeStruct(value.shape, value.dtype),
        in_specs=[pl.BlockSpec(memory_space=pl.ANY)] * (1 + len(first)),
        out_specs=pl.BlockSpec(memory_space=pl.ANY),
        input_output_aliases={0: 0},
    )(value, *first)


def nt(a, b):
    return lax.dot_general(a, b, (((1,), (1,)), ((), ())), preferred_element_type=F32)


def nn(a, b):
    return lax.dot_general(a, b, (((1,), (0,)), ((), ())), preferred_element_type=F32)


def tn(a, b):
    return lax.dot_general(a, b, (((0,), (0,)), ((), ())), preferred_element_type=F32)


def both(ref, start, rows):
    return [ref[start : start + rows, :], ref[2 * rows + start : 3 * rows + start, :]]


def grads(own, before, keys, heads, rows, scale, so_far=()):
    head = keys[0].shape[1] // heads
    n = len(keys)
    last = len(so_far) > 0

    def kernel(*refs):
        own_refs, before_refs, key_refs = refs[:4], refs[4:8], refs[8 : 8 + n]
        sums_in = refs[8 + n : 8 + n + len(so_far)]
        out_keys, (out_own, out_before) = refs[-2 - n : -2], refs[-2:]
        k = jnp.concatenate(sum((both(r, 0, rows) for r in key_refs), []), axis=0)
        v = jnp.concatenate(sum((both(r, rows, rows) for r in key_refs), []), axis=0)
        grad_k = grad_v = None
        for side, (out_ref, sources) in enumerate(((out_own, own_refs), (out_before, before_refs))):
            for half in range(2):
                pair = sources[2 * half : 2 * half + 2]
                q = jnp.concatenate(sum((both(r, 0, rows) for r in pair), []), axis=0)
                g = jnp.concatenate(sum((both(r, rows, rows) for r in pair), []), axis=0)
                stats = [
                    r[4 * rows + e * (PAD // 2) : 4 * rows + e * (PAD // 2) + 1, :].astype(F32)
                    for r in pair
                    for e in range(2)
                ]
                sums = jnp.concatenate([s[:, :rows] for s in stats], axis=1)
                deltas = jnp.concatenate([s[:, rows:] for s in stats], axis=1)
                prob = jnp.exp(nt(k, q) * scale - sums)
                gv = nn(prob.astype(LOW), g)
                score_grad = (prob * (nt(v, g) - deltas)).astype(LOW)
                gk = nn(score_grad, q)
                grad_k = gk if grad_k is None else grad_k + gk
                grad_v = gv if grad_v is None else grad_v + gv
                gq = tn(score_grad, k) * scale
                at = slice(half * 4 * rows, (half + 1) * 4 * rows)
                if last:
                    gq = gq + sums_in[side][at, :]
                out_ref[at, :] = gq.astype(out_ref.dtype)
        grad_k = (grad_k * scale).astype(LOW)
        grad_v = grad_v.astype(LOW)
        for d in range(n):
            for e in range(2):
                at = (2 * d + e) * rows
                out_keys[d][2 * e * rows : (2 * e + 1) * rows, :] = grad_k[at : at + rows]
                out_keys[d][(2 * e + 1) * rows : (2 * e + 2) * rows, :] = grad_v[at : at + rows]

    width = keys[0].shape[1]
    query_block = pl.BlockSpec((4 * rows + PAD, head), lambda h: (0, h))
    key_block = pl.BlockSpec((4 * rows, head), lambda h: (0, h))
    total = pl.BlockSpec((8 * rows, head), lambda h: (0, h))
    pairs = heads * (2 * n * rows) * (16 * rows)
    out = pl.pallas_call(
        kernel,
        grid=(heads,),
        in_specs=[query_block] * 8 + [key_block] * n + [total] * len(so_far),
        out_specs=[key_block] * n + [total, total],
        out_shape=[jax.ShapeDtypeStruct((4 * rows, width), LOW)] * n
        + [
            jax.ShapeDtypeStruct((8 * rows, width), F32),
            jax.ShapeDtypeStruct((8 * rows, width), LOW if last else F32),
        ],
        compiler_params=pltpu.CompilerParams(
            dimension_semantics=("arbitrary",), vmem_limit_bytes=40 << 20
        ),
        cost_estimate=pl.CostEstimate(
            flops=10 * pairs * head, bytes_accessed=8 << 20, transcendentals=pairs
        ),
    )(*own, *before, *keys, *so_far)
    return out[:n], out[n], out[n + 1]


def query_sums(own, returned, rows):
    def kernel(own_ref, back_ref, *outs):
        for d in range(CHIPS):
            at = slice(2 * d * rows, (2 * d + 2) * rows)
            outs[d][...] = (own_ref[at, :] + back_ref[at, :].astype(F32)).astype(LOW)

    return pl.pallas_call(
        kernel,
        out_shape=[jax.ShapeDtypeStruct((2 * rows, own.shape[1]), LOW)] * CHIPS,
        in_specs=whole(2),
        out_specs=whole(CHIPS),
        compiler_params=pltpu.CompilerParams(vmem_limit_bytes=32 << 20),
    )(own, returned)


def cross_parts(parts, rows):
    shape = jax.ShapeDtypeStruct((CHIPS, parts[0].shape[0] // 2, parts[0].shape[1]), LOW)

    def kernel(*refs):
        half = shape.shape[1]
        for d in range(CHIPS):
            refs[-1][d] = refs[d][half:]

    return pl.pallas_call(
        kernel,
        out_shape=shape,
        in_specs=whole(CHIPS),
        out_specs=whole(1)[0],
        compiler_params=pltpu.CompilerParams(vmem_limit_bytes=32 << 20),
    )(*parts)


def spread(parts, other, place, rows, count):
    width = parts[0].shape[1]

    def kernel(place_ref, *refs):
        other_ref, outs = refs[CHIPS], refs[CHIPS + 1 :]
        for d in range(CHIPS):
            chip = 2 * lax.rem(place_ref[0] + d, CHIPS)
            for i in range(count):
                at = slice(i * rows, (i + 1) * rows)
                outs[i][:, columns(chip + place_ref[1], width)] = refs[d][at]
                outs[i][:, columns(chip + 1 - place_ref[1], width)] = other_ref[d, at]

    shape = [jax.ShapeDtypeStruct((rows, 8 * width), LOW)] * count
    return call(kernel, shape, place, *parts, other)


def per_device(blocks, query_rows, key_rows, value_rows, out_grad, log_sums, deltas):
    rows, heads_total = log_sums.shape
    heads = heads_total // 8
    width = query_rows.shape[1] // 8
    scale = (width // heads) ** (-0.5)
    me = lax.axis_index("uly")
    place = jnp.stack([me // 2, me % 2]).astype(jnp.int32)
    stats = jnp.concatenate([log_sums.T, deltas.T], axis=1).reshape(8, 1, width)
    stats = jnp.pad(stats, ((0, 0), (0, PAD - 1), (0, 0)))

    cores = core_pairs(blocks)
    there = [gather_pairs(blocks, d) for d in range(CHIPS)]
    home = [back(pairs) for pairs in there]
    onward = next_pairs(blocks)

    other = moved(other_core_parts(query_rows, out_grad, stats, place), cores)
    sent = messages(query_rows, out_grad, stats, other, place)
    own = [moved(m, there[d]) for d, m in enumerate(sent)]
    before = [moved(m, onward) for m in own]

    other = moved(other_core_parts(key_rows, value_rows, None, place), cores)
    sent = messages(key_rows, value_rows, None, other, place)
    sent = [
        sent[0],
        held(sent[1], own[1], own[3], *(before[1],)),
        held(sent[2], own[2], *(before[3],)),
        held(sent[3], own[1], own[3], *(before[1],)),
    ]
    keys = [moved(m, there[d]) for d, m in enumerate(sent)]

    first, own_query, cross_query = grads(own, before, (keys[0], keys[1]), heads, rows, scale)
    second, own_query, cross_query = grads(
        own, before, (keys[3], keys[2]), heads, rows, scale, (own_query, cross_query)
    )
    key_grads = (first[0], first[1], second[1], second[0])
    returned = moved(cross_query, back(onward))
    key_home = [moved(m, home[d]) for d, m in enumerate(key_grads)]
    query_grads = query_sums(own_query, returned, rows)
    query_home = [moved(m, home[d]) for d, m in enumerate(query_grads)]

    other = moved(cross_parts(key_home, rows), cores)
    out_k, out_v = spread(key_home, other, place, rows, 2)
    other = moved(cross_parts(query_home, rows), cores)
    (out_q,) = spread(query_home, other, place, rows, 1)
    return out_q, out_k, out_v


def solution(mesh):
    rows = P(AXES, None)
    return jax.shard_map(
        functools.partial(per_device, mesh.shape["blk"]),
        mesh=mesh,
        in_specs=(rows,) * 6,
        out_specs=(rows,) * 3,
        check_vma=False,
    )
```

```python
import functools

import jax
import jax.numpy as jnp
from jax import lax
from jax.experimental import pallas as pl
from jax.experimental.pallas import tpu as pltpu
from jax.sharding import PartitionSpec as P

F32 = jnp.float32
LOW = jnp.bfloat16
AXES = ("blk", "uly")
CHIPS = 4
RING = 8
PAD = 16


def shift(b, core):
    return (b // RING % 2) * core


def gather_pairs(blocks, d):
    return [(b * 8 + u, b * 8 + (u + 2 * d) % 8) for b in range(blocks) for u in range(8)]


def next_pairs(blocks):
    pairs = []
    for b in range(blocks):
        after = (b + 1) % blocks
        for u in range(8):
            chip, core = u // 2, u % 2
            chip = (chip + shift(b, core) - shift(after, core)) % CHIPS
            pairs.append((b * 8 + u, after * 8 + 2 * chip + core))
    return pairs


def hop_pairs(blocks):
    pairs = []
    for s, t in next_pairs(blocks):
        b = s // 8
        pairs.append((s, (b ^ RING) * 8 + t % 8 if b % RING == RING - 1 else s))
    return pairs


def after_hop_pairs(blocks):
    onward = dict(next_pairs(blocks))
    return [(t, onward[s]) for s, t in hop_pairs(blocks)]


def back(pairs):
    return [(t, s) for s, t in pairs]


def core_pairs(blocks):
    return [(i, i ^ 1) for i in range(blocks * 8)]


def moved(value, pairs):
    if all(s == t for s, t in pairs):
        return value
    return lax.ppermute(value, AXES, pairs)


def whole(n):
    return [pl.BlockSpec(memory_space=pltpu.VMEM)] * n


def columns(group, width):
    return pl.ds(pl.multiple_of(group * width, 128), width)


def call(kernel, out_shape, place, *arrays, after=()):
    moved_bytes = sum(a.size * a.dtype.itemsize for a in arrays)
    outs = out_shape if isinstance(out_shape, (list, tuple)) else [out_shape]
    moved_bytes += sum(o.size * o.dtype.itemsize for o in outs)
    waits = len(after)

    def body(place_ref, *refs):
        kernel(place_ref, *refs[waits:])

    return pl.pallas_call(
        body,
        out_shape=out_shape,
        in_specs=[pl.BlockSpec(memory_space=pltpu.SMEM)]
        + [pl.BlockSpec(memory_space=pl.ANY)] * waits
        + whole(len(arrays)),
        out_specs=jax.tree.map(lambda _: pl.BlockSpec(memory_space=pltpu.VMEM), out_shape),
        compiler_params=pltpu.CompilerParams(vmem_limit_bytes=32 << 20),
        cost_estimate=pl.CostEstimate(flops=0, bytes_accessed=moved_bytes, transcendentals=0),
    )(place, *after, *arrays)


def joined(parts, place, after=()):
    length, width = parts[0].shape

    def kernel(place_ref, *refs):
        for i in range(len(parts)):
            refs[-1][i * length : (i + 1) * length] = refs[i][...]

    return call(kernel, jax.ShapeDtypeStruct((len(parts) * length, width), LOW), place, *parts, after=after)


def other_core_parts(first, second, stats, place):
    rows, width = first.shape[0], first.shape[1] // 8
    extra = PAD if stats is not None else 0

    def kernel(place_ref, a_ref, b_ref, *refs):
        out_ref = refs[-1]
        for d in range(CHIPS):
            group = 2 * lax.rem(place_ref[1] + d, CHIPS) + 1 - place_ref[2]
            out_ref[d, :rows] = a_ref[:, columns(group, width)]
            out_ref[d, rows : 2 * rows] = b_ref[:, columns(group, width)]
            if extra:
                out_ref[d, 2 * rows :] = refs[0][group]

    arrays = (first, second) + ((stats,) if extra else ())
    shape = jax.ShapeDtypeStruct((CHIPS, 2 * rows + extra, width), LOW)
    return call(kernel, shape, place, *arrays)


def messages(first, second, stats, other, place, which, after=()):
    rows, width = first.shape[0], first.shape[1] // 8
    extra = PAD if stats is not None else 0

    def kernel(place_ref, a_ref, b_ref, *refs):
        other_ref, outs = refs[-len(which) - 1], refs[-len(which) :]
        for d, out_ref in zip(which, outs):
            group = 2 * lax.rem(place_ref[0] + d, CHIPS) + place_ref[2]
            out_ref[:rows] = a_ref[:, columns(group, width)]
            out_ref[rows : 2 * rows] = b_ref[:, columns(group, width)]
            out_ref[2 * rows : 4 * rows] = other_ref[d, : 2 * rows]
            if extra:
                out_ref[4 * rows :] = jnp.concatenate(
                    [refs[0][group, : PAD // 2], other_ref[d, 2 * rows : 2 * rows + PAD // 2]], axis=0
                )

    arrays = (first, second) + ((stats,) if extra else ()) + (other,)
    shape = [jax.ShapeDtypeStruct((4 * rows + extra, width), LOW)] * len(which)
    return call(kernel, shape, place, *arrays, after=after)


def nt(a, b):
    return lax.dot_general(a, b, (((1,), (1,)), ((), ())), preferred_element_type=F32)


def nn(a, b):
    return lax.dot_general(a, b, (((1,), (0,)), ((), ())), preferred_element_type=F32)


def tn(a, b):
    return lax.dot_general(a, b, (((0,), (0,)), ((), ())), preferred_element_type=F32)


def grads(queries, keys, work, sums_in, outputs, rows, heads, scale):
    width = keys[0].shape[1]
    head = width // heads
    size = 4 * rows + PAD
    ins, outs = list(sums_in), list(outputs)

    def kernel(*refs):
        query_refs = refs[: len(queries)]
        key_refs = refs[len(queries) : len(queries) + len(keys)]
        in_refs = dict(zip(ins, refs[len(queries) + len(keys) :]))
        out_refs = dict(zip(outs, refs[len(queries) + len(keys) + len(ins) :]))
        def part(ref, top, which):
            starts = [top + (2 * e + which) * rows for e in range(2)]
            return [ref[t : t + rows] for t in starts]

        total = {}
        for (kind, i), ref in in_refs.items():
            if kind == "q":
                total[kind, i] = ref[...]
            else:
                total["k", i] = jnp.concatenate(part(ref, 0, 0), axis=0)
                total["v", i] = jnp.concatenate(part(ref, 0, 1), axis=0)

        def add(kind, i, value):
            total[kind, i] = total[kind, i] + value if (kind, i) in total else value

        def rows_of(refs, tops, which):
            return jnp.concatenate([x for r in refs for t in tops for x in part(r, t, which)], axis=0)

        for queries_here, keys_here in work:
            sources = [query_refs[i] for i in queries_here]
            q = rows_of(sources, (0, size), 0)
            g = rows_of(sources, (0, size), 1)
            stats = []
            for ref in sources:
                for top in (0, size):
                    pad = ref[top + 4 * rows : top + size].astype(F32)
                    stats += [pad[:1], pad[PAD // 2 : PAD // 2 + 1]]
            sums = jnp.concatenate([s[:, :rows] for s in stats], axis=1)
            deltas = jnp.concatenate([s[:, rows:] for s in stats], axis=1)
            k = rows_of([key_refs[d] for d in keys_here], (0,), 0)
            v = rows_of([key_refs[d] for d in keys_here], (0,), 1)
            prob = jnp.exp(nt(k, q) * scale - sums)
            score_grad = (prob * (nt(v, g) - deltas)).astype(LOW)
            gv = nn(prob.astype(LOW), g)
            gk = nn(score_grad, q)
            gq = tn(score_grad, k)
            for n, d in enumerate(keys_here):
                at = slice(2 * n * rows, 2 * (n + 1) * rows)
                add("k", d, gk[at])
                add("v", d, gv[at])
            for n, i in enumerate(queries_here):
                add("q", i, gq[4 * n * rows : 4 * (n + 1) * rows])
        for (kind, i), ref in out_refs.items():
            by = scale if ref.dtype == LOW else 1.0
            if kind == "q":
                ref[...] = (total[kind, i] * by).astype(ref.dtype)
                continue
            for e in range(2):
                at = slice(e * rows, (e + 1) * rows)
                ref[2 * e * rows : (2 * e + 1) * rows] = (total["k", i][at] * by).astype(ref.dtype)
                ref[(2 * e + 1) * rows : (2 * e + 2) * rows] = total["v", i][at].astype(ref.dtype)

    def block(length):
        return pl.BlockSpec((length, head), lambda h: (0, h))

    shapes = [jax.ShapeDtypeStruct((4 * rows, width), outputs[name]) for name in outs]
    pairs = heads * 8 * rows * rows * sum(len(a) * len(b) for a, b in work)
    results = pl.pallas_call(
        kernel,
        grid=(heads,),
        in_specs=[block(2 * size)] * len(queries) + [block(4 * rows)] * (len(keys) + len(ins)),
        out_specs=[block(4 * rows)] * len(outs),
        out_shape=shapes,
        compiler_params=pltpu.CompilerParams(
            dimension_semantics=("arbitrary",), vmem_limit_bytes=40 << 20
        ),
        cost_estimate=pl.CostEstimate(
            flops=10 * pairs * head, bytes_accessed=8 << 20, transcendentals=pairs
        ),
    )(*queries, *keys, *sums_in.values())
    return dict(zip(outs, results))


def query_sums(own, returned, rows, scale, place):
    def kernel(place_ref, own_ref, back_ref, *outs):
        for i in range(2):
            at = slice(2 * i * rows, (2 * i + 2) * rows)
            outs[i][...] = (own_ref[at, :] * scale + back_ref[at, :].astype(F32)).astype(LOW)

    shape = [jax.ShapeDtypeStruct((2 * rows, own.shape[1]), LOW)] * 2
    return call(kernel, shape, place, own, returned)


def cross_parts(parts, place, after=()):
    shape = jax.ShapeDtypeStruct((CHIPS, parts[0].shape[0] // 2, parts[0].shape[1]), LOW)

    def kernel(place_ref, *refs):
        half = shape.shape[1]
        for d in range(CHIPS):
            refs[-1][d] = refs[d][half:]

    return call(kernel, shape, place, *parts, after=after)


def spread(parts, other, place, rows, count):
    width = parts[0].shape[1]

    def kernel(place_ref, *refs):
        other_ref, outs = refs[CHIPS], refs[CHIPS + 1 :]
        for d in range(CHIPS):
            mine = 2 * lax.rem(place_ref[0] + d, CHIPS) + place_ref[2]
            others = 2 * lax.rem(place_ref[1] + d, CHIPS) + 1 - place_ref[2]
            for i in range(count):
                at = slice(i * rows, (i + 1) * rows)
                outs[i][:, columns(mine, width)] = refs[d][at]
                outs[i][:, columns(others, width)] = other_ref[d, at]

    shape = [jax.ShapeDtypeStruct((rows, 8 * width), LOW)] * count
    return call(kernel, shape, place, *parts, other)


def per_device(blocks, query_rows, key_rows, value_rows, out_grad, log_sums, deltas):
    rows, heads_total = log_sums.shape
    heads = heads_total // 8
    width = query_rows.shape[1] // 8
    scale = (width // heads) ** (-0.5)
    chip, core = lax.axis_index("uly") // 2, lax.axis_index("uly") % 2
    block = lax.axis_index("blk")
    place = jnp.stack([chip + shift(block, core), chip + shift(block, 1 - core), core]).astype(jnp.int32)
    stats = jnp.concatenate([log_sums.T, deltas.T], axis=1).reshape(8, 1, width)
    stats = jnp.pad(stats, ((0, 0), (0, PAD - 1), (0, 0)))

    cores = core_pairs(blocks)
    there = [gather_pairs(blocks, d) for d in range(CHIPS)]
    home = [back(pairs) for pairs in there]
    onward = next_pairs(blocks)
    hop, after_hop = hop_pairs(blocks), after_hop_pairs(blocks)

    other = moved(other_core_parts(query_rows, out_grad, stats, place), cores)
    other_keys = moved(other_core_parts(key_rows, value_rows, None, place), cores)
    sent = messages(query_rows, out_grad, stats, other, place, range(CHIPS))
    own = [moved(m, there[d]) for d, m in enumerate(sent)]
    queries = [joined((own[0], own[1]), place)]
    before = [moved(queries[0], onward)]

    near = messages(key_rows, value_rows, None, other_keys, place, (1, 3), ())
    near_keys = [moved(m, there[d]) for d, m in zip((1, 3), near)]
    queries.append(joined((own[3], own[2]), place, tuple(near_keys)))
    before.append(moved(queries[1], onward))
    rest = messages(key_rows, value_rows, None, other_keys, place, (0, 2), (own[1],))
    keys = [rest[0], near_keys[0], moved(rest[1], there[2]), near_keys[1]]

    early = (0, 1, 3)
    mine = [("q", 0), ("q", 1), ("q", 2)]
    so_far = grads(
        [*queries, before[0]], [keys[d] for d in early], [((i,), (0, 1, 2)) for i in range(3)],
        {}, {name: F32 for name in mine + [("kv", 0), ("kv", 1), ("kv", 2)]}, rows, heads, scale,
    )
    more = grads(
        [before[1]], [keys[d] for d in early], [((0,), (0, 1, 2))],
        {("kv", n): so_far["kv", n] for n in range(3)},
        {("q", 0): F32, ("kv", 0): LOW, ("kv", 1): LOW, ("kv", 2): LOW}, rows, heads, scale,
    )
    last = grads(
        [*queries, *before], [keys[2]], [((0, 1), (0,)), ((2, 3), (0,))],
        {**{name: so_far[name] for name in mine}, ("q", 3): more["q", 0]},
        {("q", 0): F32, ("q", 1): F32, ("q", 2): LOW, ("q", 3): LOW, ("kv", 0): LOW}, rows, heads, scale,
    )
    key_grads = [more["kv", 0], more["kv", 1], last["kv", 0], more["kv", 2]]
    done = last
    returned = [
        moved(done["q", 2], back(onward)),
        moved(done["q", 3], back(onward)),
    ]
    key_home = [moved(m, home[d]) for d, m in enumerate(key_grads)]
    grad_0, grad_1 = query_sums(done["q", 0], returned[0], rows, scale, place)
    grad_3, grad_2 = query_sums(done["q", 1], returned[1], rows, scale, place)
    query_home = [moved(m, home[d]) for d, m in enumerate((grad_0, grad_1, grad_2, grad_3))]

    other = moved(cross_parts(key_home, place, tuple(query_home[1:])), cores)
    out_k, out_v = spread(key_home, other, place, rows, 2)
    other = moved(cross_parts(query_home, place), cores)
    (out_q,) = spread(query_home, other, place, rows, 1)
    return out_q, out_k, out_v


def solution(mesh):
    rows = P(AXES, None)
    return jax.shard_map(
        functools.partial(per_device, mesh.shape["blk"]),
        mesh=mesh,
        in_specs=(rows,) * 6,
        out_specs=(rows,) * 3,
        check_vma=False,
    )
```

```python
import functools

import jax
import jax.numpy as jnp
from jax import lax
from jax.experimental import pallas as pl
from jax.experimental.pallas import tpu as pltpu
from jax.sharding import PartitionSpec as P

F32 = jnp.float32
LOW = jnp.bfloat16
AXES = ("blk", "uly")
CHIPS = 4
RING = 8
PAD = 8


def shift(b, core):
    return (b // RING % 2) * core


def gather_pairs(blocks, d):
    return [(b * 8 + u, b * 8 + (u + 2 * d) % 8) for b in range(blocks) for u in range(8)]


def next_pairs(blocks):
    pairs = []
    for b in range(blocks):
        after = (b + 1) % blocks
        for u in range(8):
            chip, core = u // 2, u % 2
            chip = (chip + shift(b, core) - shift(after, core)) % CHIPS
            pairs.append((b * 8 + u, after * 8 + 2 * chip + core))
    return pairs


def back(pairs):
    return [(t, s) for s, t in pairs]


def core_pairs(blocks):
    return [(i, i ^ 1) for i in range(blocks * 8)]


def moved(value, pairs):
    if all(s == t for s, t in pairs):
        return value
    return lax.ppermute(value, AXES, pairs)


def whole(n):
    return [pl.BlockSpec(memory_space=pltpu.VMEM)] * n


def columns(group, width):
    return pl.ds(pl.multiple_of(group * width, 128), width)


def call(kernel, out_shape, place, *arrays, after=()):
    moved_bytes = sum(a.size * a.dtype.itemsize for a in arrays)
    outs = out_shape if isinstance(out_shape, (list, tuple)) else [out_shape]
    moved_bytes += sum(o.size * o.dtype.itemsize for o in outs)
    waits = len(after)

    def body(place_ref, *refs):
        kernel(place_ref, *refs[waits:])

    return pl.pallas_call(
        body,
        out_shape=out_shape,
        in_specs=[pl.BlockSpec(memory_space=pltpu.SMEM)]
        + [pl.BlockSpec(memory_space=pl.ANY)] * waits
        + whole(len(arrays)),
        out_specs=jax.tree.map(lambda _: pl.BlockSpec(memory_space=pltpu.VMEM), out_shape),
        compiler_params=pltpu.CompilerParams(vmem_limit_bytes=32 << 20),
        cost_estimate=pl.CostEstimate(flops=0, bytes_accessed=moved_bytes, transcendentals=0),
    )(place, *after, *arrays)


def joined(parts, place, after=()):
    length, width = parts[0].shape

    def kernel(place_ref, *refs):
        for i in range(len(parts)):
            refs[-1][i * length : (i + 1) * length] = refs[i][...]

    return call(kernel, jax.ShapeDtypeStruct((len(parts) * length, width), LOW), place, *parts, after=after)


def other_core_parts(first, second, stats, place):
    rows, width = first.shape[0], first.shape[1] // 8
    extra = PAD if stats is not None else 0

    def kernel(place_ref, a_ref, b_ref, *refs):
        out_ref = refs[-1]
        for d in range(CHIPS):
            group = 2 * lax.rem(place_ref[1] + d, CHIPS) + 1 - place_ref[2]
            out_ref[d, :rows] = a_ref[:, columns(group, width)]
            out_ref[d, rows : 2 * rows] = b_ref[:, columns(group, width)]
            if extra:
                out_ref[d, 2 * rows :] = refs[0][group]

    arrays = (first, second) + ((stats,) if extra else ())
    shape = jax.ShapeDtypeStruct((CHIPS, 2 * rows + extra, width), LOW)
    return call(kernel, shape, place, *arrays)


def messages(first, second, stats, other, place, which, after=()):
    rows, width = first.shape[0], first.shape[1] // 8
    extra = PAD if stats is not None else 0

    def kernel(place_ref, a_ref, b_ref, *refs):
        other_ref, outs = refs[-len(which) - 1], refs[-len(which) :]
        for d, out_ref in zip(which, outs):
            group = 2 * lax.rem(place_ref[0] + d, CHIPS) + place_ref[2]
            out_ref[:rows] = a_ref[:, columns(group, width)]
            out_ref[rows : 2 * rows] = b_ref[:, columns(group, width)]
            out_ref[2 * rows : 4 * rows] = other_ref[d, : 2 * rows]
            if extra:
                out_ref[4 * rows :] = jnp.concatenate(
                    [refs[0][group, : PAD // 2], other_ref[d, 2 * rows : 2 * rows + PAD // 2]], axis=0
                )

    arrays = (first, second) + ((stats,) if extra else ()) + (other,)
    shape = [jax.ShapeDtypeStruct((4 * rows + extra, width), LOW)] * len(which)
    return call(kernel, shape, place, *arrays, after=after)


def nt(a, b):
    return lax.dot_general(a, b, (((1,), (1,)), ((), ())), preferred_element_type=F32)


def nn(a, b):
    return lax.dot_general(a, b, (((1,), (0,)), ((), ())), preferred_element_type=F32)


def tn(a, b):
    return lax.dot_general(a, b, (((0,), (0,)), ((), ())), preferred_element_type=F32)


def grads(queries, keys, work, sums_in, outputs, rows, heads, scale):
    width = keys[0].shape[1]
    head = width // heads
    size = 4 * rows + PAD
    ins, outs = list(sums_in), list(outputs)

    def kernel(*refs):
        query_refs = refs[: len(queries)]
        key_refs = refs[len(queries) : len(queries) + len(keys)]
        in_refs = dict(zip(ins, refs[len(queries) + len(keys) :]))
        out_refs = dict(zip(outs, refs[len(queries) + len(keys) + len(ins) :]))
        def part(ref, top, which):
            starts = [top + (2 * e + which) * rows for e in range(2)]
            return [ref[t : t + rows] for t in starts]

        total = {}
        for (kind, i), ref in in_refs.items():
            if kind == "q":
                total[kind, i] = ref[...]
            else:
                total["k", i] = jnp.concatenate(part(ref, 0, 0), axis=0)
                total["v", i] = jnp.concatenate(part(ref, 0, 1), axis=0)

        def add(kind, i, value):
            total[kind, i] = total[kind, i] + value if (kind, i) in total else value

        def rows_of(refs, tops, which):
            return jnp.concatenate([x for r in refs for t in tops for x in part(r, t, which)], axis=0)

        for queries_here, keys_here in work:
            sources = [query_refs[i] for i in queries_here]
            q = rows_of(sources, (0, size), 0)
            g = rows_of(sources, (0, size), 1)
            stats = []
            for ref in sources:
                for top in (0, size):
                    pad = ref[top + 4 * rows : top + size].astype(F32)
                    stats += [pad[:1], pad[PAD // 2 : PAD // 2 + 1]]
            sums = jnp.concatenate([s[:, :rows] for s in stats], axis=1)
            deltas = jnp.concatenate([s[:, rows:] for s in stats], axis=1)
            k = rows_of([key_refs[d] for d in keys_here], (0,), 0)
            v = rows_of([key_refs[d] for d in keys_here], (0,), 1)
            prob = jnp.exp(nt(k, q) * scale - sums)
            score_grad = (prob * (nt(v, g) - deltas)).astype(LOW)
            gv = nn(prob.astype(LOW), g)
            gk = nn(score_grad, q)
            gq = tn(score_grad, k)
            for n, d in enumerate(keys_here):
                at = slice(2 * n * rows, 2 * (n + 1) * rows)
                add("k", d, gk[at])
                add("v", d, gv[at])
            for n, i in enumerate(queries_here):
                add("q", i, gq[4 * n * rows : 4 * (n + 1) * rows])
        for (kind, i), ref in out_refs.items():
            by = scale if ref.dtype == LOW else 1.0
            if kind == "q":
                ref[...] = (total[kind, i] * by).astype(ref.dtype)
                continue
            for e in range(2):
                at = slice(e * rows, (e + 1) * rows)
                ref[2 * e * rows : (2 * e + 1) * rows] = (total["k", i][at] * by).astype(ref.dtype)
                ref[(2 * e + 1) * rows : (2 * e + 2) * rows] = total["v", i][at].astype(ref.dtype)

    def block(length):
        return pl.BlockSpec((length, head), lambda h: (0, h))

    shapes = [jax.ShapeDtypeStruct((4 * rows, width), outputs[name]) for name in outs]
    pairs = heads * 8 * rows * rows * sum(len(a) * len(b) for a, b in work)
    results = pl.pallas_call(
        kernel,
        grid=(heads,),
        in_specs=[block(2 * size)] * len(queries) + [block(4 * rows)] * (len(keys) + len(ins)),
        out_specs=[block(4 * rows)] * len(outs),
        out_shape=shapes,
        compiler_params=pltpu.CompilerParams(
            dimension_semantics=("arbitrary",), vmem_limit_bytes=40 << 20
        ),
        cost_estimate=pl.CostEstimate(
            flops=10 * pairs * head, bytes_accessed=8 << 20, transcendentals=pairs
        ),
    )(*queries, *keys, *sums_in.values())
    return dict(zip(outs, results))


def query_sums(own, returned, rows, scale, place):
    def kernel(place_ref, own_ref, back_ref, *outs):
        for i in range(2):
            at = slice(2 * i * rows, (2 * i + 2) * rows)
            outs[i][...] = (own_ref[at, :] * scale + back_ref[at, :].astype(F32)).astype(LOW)

    shape = [jax.ShapeDtypeStruct((2 * rows, own.shape[1]), LOW)] * 2
    return call(kernel, shape, place, own, returned)


def cross_parts(parts, place, after=()):
    shape = jax.ShapeDtypeStruct((CHIPS, parts[0].shape[0] // 2, parts[0].shape[1]), LOW)

    def kernel(place_ref, *refs):
        half = shape.shape[1]
        for d in range(CHIPS):
            refs[-1][d] = refs[d][half:]

    return call(kernel, shape, place, *parts, after=after)


def spread(parts, other, place, rows, count):
    width = parts[0].shape[1]

    def kernel(place_ref, *refs):
        other_ref, outs = refs[CHIPS], refs[CHIPS + 1 :]
        for d in range(CHIPS):
            mine = 2 * lax.rem(place_ref[0] + d, CHIPS) + place_ref[2]
            others = 2 * lax.rem(place_ref[1] + d, CHIPS) + 1 - place_ref[2]
            for i in range(count):
                at = slice(i * rows, (i + 1) * rows)
                outs[i][:, columns(mine, width)] = refs[d][at]
                outs[i][:, columns(others, width)] = other_ref[d, at]

    shape = [jax.ShapeDtypeStruct((rows, 8 * width), LOW)] * count
    return call(kernel, shape, place, *parts, other)


def per_device(blocks, query_rows, key_rows, value_rows, out_grad, log_sums, deltas):
    rows, heads_total = log_sums.shape
    heads = heads_total // 8
    width = query_rows.shape[1] // 8
    scale = (width // heads) ** (-0.5)
    chip, core = lax.axis_index("uly") // 2, lax.axis_index("uly") % 2
    block = lax.axis_index("blk")
    place = jnp.stack([chip + shift(block, core), chip + shift(block, 1 - core), core]).astype(jnp.int32)
    stats = jnp.concatenate([log_sums.T, deltas.T], axis=1).reshape(8, 1, width)
    stats = jnp.pad(stats, ((0, 0), (0, PAD - 1), (0, 0)))

    cores = core_pairs(blocks)
    there = [gather_pairs(blocks, d) for d in range(CHIPS)]
    home = [back(pairs) for pairs in there]
    onward = next_pairs(blocks)

    other = moved(other_core_parts(query_rows, out_grad, stats, place), cores)
    other_keys = moved(other_core_parts(key_rows, value_rows, None, place), cores)
    sent = messages(query_rows, out_grad, stats, other, place, range(CHIPS))
    own = [moved(m, there[d]) for d, m in enumerate(sent)]
    queries = [joined((own[0], own[1]), place)]
    before = [moved(queries[0], onward)]

    near = messages(key_rows, value_rows, None, other_keys, place, (1, 3), ())
    near_keys = [moved(m, there[d]) for d, m in zip((1, 3), near)]
    queries.append(joined((own[3], own[2]), place, tuple(near_keys)))
    before.append(moved(queries[1], onward))
    rest = messages(key_rows, value_rows, None, other_keys, place, (0, 2), (own[1],))
    keys = [rest[0], near_keys[0], moved(rest[1], there[2]), near_keys[1]]

    early = (0, 1, 3)
    mine = [("q", 0), ("q", 1), ("q", 2)]
    so_far = grads(
        [*queries, before[0]], [keys[d] for d in early], [((i,), (0, 1, 2)) for i in range(3)],
        {}, {name: F32 for name in mine + [("kv", 0), ("kv", 1), ("kv", 2)]}, rows, heads, scale,
    )
    more = grads(
        [before[1]], [keys[d] for d in early], [((0,), (0, 1, 2))],
        {("kv", n): so_far["kv", n] for n in range(3)},
        {("q", 0): F32, ("kv", 0): LOW, ("kv", 1): LOW, ("kv", 2): LOW}, rows, heads, scale,
    )
    last = grads(
        [*queries, *before], [keys[2]], [((0, 1), (0,)), ((2, 3), (0,))],
        {**{name: so_far[name] for name in mine}, ("q", 3): more["q", 0]},
        {("q", 0): F32, ("q", 1): F32, ("q", 2): LOW, ("q", 3): LOW, ("kv", 0): LOW}, rows, heads, scale,
    )
    key_grads = [more["kv", 0], more["kv", 1], last["kv", 0], more["kv", 2]]
    done = last
    returned = [
        moved(done["q", 2], back(onward)),
        moved(done["q", 3], back(onward)),
    ]
    key_home = [moved(m, home[d]) for d, m in enumerate(key_grads)]
    grad_0, grad_1 = query_sums(done["q", 0], returned[0], rows, scale, place)
    grad_3, grad_2 = query_sums(done["q", 1], returned[1], rows, scale, place)
    query_home = [moved(m, home[d]) for d, m in enumerate((grad_0, grad_1, grad_2, grad_3))]

    other = moved(cross_parts(key_home, place, tuple(query_home[1:])), cores)
    out_k, out_v = spread(key_home, other, place, rows, 2)
    other = moved(cross_parts(query_home, place), cores)
    (out_q,) = spread(query_home, other, place, rows, 1)
    return out_q, out_k, out_v


def solution(mesh):
    rows = P(AXES, None)
    return jax.shard_map(
        functools.partial(per_device, mesh.shape["blk"]),
        mesh=mesh,
        in_specs=(rows,) * 6,
        out_specs=(rows,) * 3,
        check_vma=False,
    )
```
